32 devices in a mesh: groups: 2 (over y), gx: 16 (over z, x, core).
Axes of the slice: x: 2, y: 2, z: 4, core: 2. Of those that a mesh axis runs over, the one named last changes fastest.
Arguments:
- attention: bfloat16 [1024, 16384], P('groups', 'gx'), parts along dimension 0, may hold values from -6 to 6
- activated: bfloat16 [1024, 26624], P('groups', 'gx'), parts along dimension 0, may hold values from -6 to 6
- residual: bfloat16 [1024, 16384], P('groups', 'gx'), parts along dimension 0, may hold values from -90 to 90
- out_tiles: bfloat16 [16, 2048, 8192], P('gx'), may hold values from -0.046875 to 0.046875
- down_tiles: bfloat16 [16, 3328, 8192], P('gx'), may hold values from -0.0390625 to 0.0390625
- norm_gain: bfloat16 [16384], P('gx'), may hold values from 0.5 to 1.5
Outputs:
- stream: bfloat16 [1024, 16384], P('groups', 'gx'), parts along dimension 0
- normed: bfloat16 [1024, 16384], P('groups', 'gx'), parts along dimension 0
The draws below stay inside these ranges and needn't reach their ends.
There are 2 independent parts, one for each index of `groups`. The reference program is written for one: setup_inputs(seed, part) draws one part's arguments, and reference() takes and returns one part's arrays. A program takes and returns all parts, laid end to end along the dimension named above; an argument that names none is the same for every part. Nothing has to cross between parts.
All inputs are finite; a program needn't handle non-finite values.
Results may differ from the reference program's by a relative error of at most 0.0049.
Values may be sent and summed in bfloat16 or wider, within the bound.
A program may use at most 320 MiB of HBM per device.

```python
import math
import jax
import jax.numpy as jnp
from jax import lax

D = 16384
FFW = 26624
TOK = 512
COLB = 8
ROWB = 2
ASH = 1024
HSH = 1664
OCOL = 8192
N_GX = 16


def draw_residual(key, part):
    key = jax.random.fold_in(key, 7)
    key_base, key_cols, key_rows = jax.random.split(key, 3)
    column = jnp.arange(D, dtype=jnp.float32) / D
    col_scale = 4.0 ** column * jax.random.uniform(key_cols, (D,), jnp.float32, 0.5, 1.5)
    row_scale = jnp.exp(jax.random.uniform(key_rows, (TOK, 1), jnp.float32, 0.0, math.log(3.0)))
    base = jnp.clip(jax.random.normal(key_base, (TOK, D), jnp.float32), -4.5, 4.5)
    return (base * row_scale * col_scale[None, :]).astype(jnp.bfloat16)


def shard_levels(stream_key, extent, cuts, low, high):
    factor_of, own = 1.0, jax.random.fold_in(stream_key, 6)
    for position, blocks in cuts:
        heights = jnp.exp(jax.random.uniform(jax.random.fold_in(own, position), (blocks,), jnp.float32, low / len(cuts), high / len(cuts)))
        factor_of = factor_of * jnp.repeat(heights, extent[position] // blocks).reshape([-1 if axis == position else 1 for axis in range(len(extent))])
    return factor_of


def gaussian(rng, extent, spread, most, shards=(), kind=jnp.bfloat16):
    gain = shard_levels(rng, extent, shards, -0.22, 0.18) if shards else 1.0
    entries = jax.random.normal(rng, extent, jnp.float32) * spread * gain
    return jnp.minimum(jnp.maximum(entries, -most), most).astype(kind)


def setup_inputs(seed: int = 0, part: int = 0) -> dict:
    key_of = jax.random.split(jax.random.key(seed), 7)
    own_keys = jax.random.split(jax.random.fold_in(key_of[6], part), 7)
    attention = gaussian(own_keys[0], (TOK, D), 1.0, 6.0, ((1, 16),))
    activated = gaussian(own_keys[1], (TOK, FFW), 1.0, 6.0, ((1, 16),))
    residual = draw_residual(jax.random.fold_in(jax.random.fold_in(key_of[6], part), 71), part)
    out_tiles = gaussian(key_of[3], (N_GX, D // COLB, OCOL), D ** -0.5, 0.046875, ((0, 16),))
    down_tiles = gaussian(key_of[4], (N_GX, ROWB * HSH, OCOL), FFW ** -0.5, 0.0390625, ((0, 16),))
    norm_gain = jnp.clip(1.0 + 0.1 * jax.random.normal(key_of[5], (D,), jnp.float32), 0.5, 1.5).astype(jnp.bfloat16)
    return dict(attention=attention, activated=activated, residual=residual, out_tiles=out_tiles, down_tiles=down_tiles, norm_gain=norm_gain)


def reference(attention, activated, residual, out_tiles, down_tiles, norm_gain):
    att_split = attention.reshape(TOK, ROWB, COLB, ASH)
    act_split = activated.reshape(TOK, ROWB, COLB, HSH)
    out_grid = out_tiles.reshape(ROWB, COLB, ROWB * ASH, OCOL)
    down_grid = down_tiles.reshape(ROWB, COLB, ROWB * HSH, OCOL)

    def column_block(tiles):
        out_group, down_group = tiles
        total = jnp.zeros((TOK, OCOL), jnp.float32)
        for column in range(COLB):
            left = att_split[:, :, column, :].reshape(TOK, ROWB * ASH)
            right = act_split[:, :, column, :].reshape(TOK, ROWB * HSH)
            total = total + jnp.dot(left, out_group[column], preferred_element_type=jnp.float32)
            total = total + jnp.dot(right, down_group[column], preferred_element_type=jnp.float32)
        return total
    blocks = lax.map(column_block, (out_grid, down_grid))
    total = jnp.transpose(blocks, (1, 0, 2)).reshape(TOK, D)
    total = total + residual.astype(jnp.float32)
    stream = total.astype(jnp.bfloat16)
    wide = stream.astype(jnp.float32)
    mean_square = lax.optimization_barrier(jnp.mean(wide * wide, axis=1, keepdims=True))
    normed = wide * lax.rsqrt(mean_square + 1e-05) * norm_gain.astype(jnp.float32)[None, :]
    return (stream, normed.astype(jnp.bfloat16))
```

```python
import functools
import jax
import jax.numpy as jnp
from jax import lax
from jax.experimental import pallas as pl
from jax.experimental.pallas import tpu as pltpu
from jax.sharding import PartitionSpec as P

D = 16384
COLB = 8
ROWS = 128
SLOTS = 5
LANES = 256
IN_FLIGHT = 1


def dot32(left, right):
    return jnp.dot(left, right, preferred_element_type=jnp.float32)


def fused_kernel(
    devices,
    att_ref, act_ref, res_ref, wo_ref, wd_ref, gain_ref,
    stream_ref, normed_ref,
    own_att, own_act, far_att, far_act, res_v, ring_o, ring_d, own_sum,
    core_out, core_in, chip_out, chip_in, kept, stream_v, normed_v, stat,
    local_sem, ring_sem, far_send, far_recv, core_send, core_recv, chip_send, chip_recv,
    stat_send, stat_recv, out_sem,
):
    tokens, width_a = own_att.shape
    width_h = own_act.shape[1]
    chunks = tokens // ROWS
    piece = kept.shape[1]
    total_blocks = COLB * (chunks + 1)
    me = lax.axis_index("gx")
    column = lax.rem(me, COLB)
    group = lax.div(me, COLB)
    facing = lax.bitwise_xor(me, COLB)

    def ring_copies(n):
        index = jnp.where(n < COLB, group, 1 - group)
        slot = lax.rem(n, SLOTS)
        owner = lax.bitwise_xor(column, COLB - 1 - lax.rem(n, COLB))
        cols = pl.ds(pl.multiple_of(owner * piece, piece), piece)
        rows_o = pl.ds(pl.multiple_of(index * width_a, width_a), width_a)
        rows_d = pl.ds(pl.multiple_of(index * width_h, width_h), width_h)
        return (
            pltpu.make_async_copy(wo_ref.at[0, rows_o, cols], ring_o.at[slot], ring_sem.at[0, slot]),
            pltpu.make_async_copy(wd_ref.at[0, rows_d, cols], ring_d.at[slot], ring_sem.at[1, slot]),
        )

    def ring_start(n):
        for copy in ring_copies(n):
            copy.start()

    def ring_wait(n):
        for copy in ring_copies(n):
            copy.wait()

    def far_copies(t):
        rows = pl.ds(pl.multiple_of(t * ROWS, ROWS), ROWS)
        return [
            pltpu.make_async_remote_copy(
                src_ref=source.at[rows], dst_ref=target.at[rows],
                send_sem=far_send.at[k, t], recv_sem=far_recv.at[k, t],
                device_id={"gx": facing}, device_id_type=pl.DeviceIdType.MESH,
            )
            for k, (source, target) in enumerate(((att_ref, far_att), (act_ref, far_act)))
        ]

    def core_copy(t, d):
        return pltpu.make_async_remote_copy(
            src_ref=core_out.at[d], dst_ref=core_in.at[t, d],
            send_sem=core_send.at[d], recv_sem=core_recv.at[t, d],
            device_id={"gx": lax.bitwise_xor(me, 1)}, device_id_type=pl.DeviceIdType.MESH,
        )

    def chip_copy(t, d):
        return pltpu.make_async_remote_copy(
            src_ref=chip_out.at[d], dst_ref=chip_in.at[t, d],
            send_sem=chip_send.at[d], recv_sem=chip_recv.at[t, d],
            device_id={"gx": lax.bitwise_xor(me, COLB - 2 - 2 * d)}, device_id_type=pl.DeviceIdType.MESH,
        )

    def stat_copy(distance):
        peer = lax.bitwise_xor(me, distance)
        return pltpu.make_async_remote_copy(
            src_ref=stat.at[0], dst_ref=stat.at[distance],
            send_sem=stat_send.at[distance], recv_sem=stat_recv.at[distance],
            device_id={"gx": peer}, device_id_type=pl.DeviceIdType.MESH,
        )

    own_copies = [
        pltpu.make_async_copy(att_ref, own_att, local_sem.at[0]),
        pltpu.make_async_copy(act_ref, own_act, local_sem.at[1]),
        pltpu.make_async_copy(res_ref, res_v, local_sem.at[2]),
    ]
    barrier = pltpu.get_barrier_semaphore()

    @pl.loop(1, devices)
    def _(distance):
        pl.semaphore_signal(
            barrier, inc=1, device_id={"gx": lax.bitwise_xor(me, distance)},
            device_id_type=pl.DeviceIdType.MESH,
        )

    for copy in own_copies:
        copy.start()
    for n in range(SLOTS):
        ring_start(n)
    pl.semaphore_wait(barrier, devices - 1)
    for t in range(IN_FLIGHT):
        for copy in far_copies(t):
            copy.start()
    for copy in own_copies:
        copy.wait()

    def refill(n):
        @pl.when(n + SLOTS < total_blocks)
        def _():
            ring_start(n + SLOTS)

    @pl.loop(0, COLB)
    def _(j):
        ring_wait(j)
        slot = lax.rem(j, SLOTS)

        @pl.loop(0, piece // LANES)
        def _(i):
            cols = pl.ds(pl.multiple_of(i * LANES, LANES), LANES)
            own_sum[j, :, cols] = dot32(own_att[...], ring_o[slot, :, cols]) + dot32(
                own_act[...], ring_d[slot, :, cols]
            )

        refill(j)

    @pl.loop(0, chunks)
    def _(t):
        rows = pl.ds(pl.multiple_of(t * ROWS, ROWS), ROWS)
        for copy in far_copies(t):
            copy.wait()

        @pl.when(t + IN_FLIGHT < chunks)
        def _():
            for copy in far_copies(t + IN_FLIGHT):
                copy.start()

        def multiply(j, write):
            n = COLB * (t + 1) + j
            ring_wait(n)
            slot = lax.rem(n, SLOTS)

            @pl.loop(0, piece // LANES)
            def _(i):
                cols = pl.ds(pl.multiple_of(i * LANES, LANES), LANES)
                write(
                    cols,
                    own_sum[j, rows, cols]
                    + dot32(far_att[rows, :], ring_o[slot, :, cols])
                    + dot32(far_act[rows, :], ring_d[slot, :, cols]),
                )

            refill(n)

        @pl.loop(0, COLB // 2)
        def _(d):
            def to_core(cols, value):
                core_out[d, :, cols] = value.astype(jnp.bfloat16)

            multiply(2 * d, to_core)
            core_copy(t, d).start()

            def keep(cols, value):
                kept[:, cols] = value

            multiply(2 * d + 1, keep)
            core_copy(t, d).wait_recv()

            @pl.when(d < COLB // 2 - 1)
            def _():
                chip_out[d] = (kept[...] + core_in[t, d].astype(jnp.float32)).astype(jnp.bfloat16)
                chip_copy(t, d).start()

        last = COLB // 2 - 1
        total = kept[...] + core_in[t, last].astype(jnp.float32) + res_v[rows].astype(jnp.float32)
        for d in range(last):
            chip_copy(t, d).wait_recv()
            total = total + chip_in[t, d].astype(jnp.float32)
        stream = total.astype(jnp.bfloat16)
        stream_v[rows] = stream
        wide = stream.astype(jnp.float32)
        square = wide * wide
        folded = square[:, :128]
        for k in range(1, piece // 128):
            folded = folded + square[:, k * 128:(k + 1) * 128]
        stat[0, t] = jnp.sum(jnp.transpose(folded), axis=0, keepdims=True)
        for d in range(last + 1):
            core_copy(t, d).wait_send()
        for d in range(last):
            chip_copy(t, d).wait_send()

    stream_out = pltpu.make_async_copy(stream_v, stream_ref, out_sem.at[0])
    stream_out.start()

    @pl.loop(1, devices)
    def _(distance):
        stat_copy(distance).start()

    @pl.loop(1, devices)
    def _(distance):
        stat_copy(distance).wait()

    summed = jnp.sum(stat[...], axis=0)
    scale = lax.rsqrt(summed / D + 1e-05)
    for t in range(chunks):
        factor = jnp.transpose(jnp.broadcast_to(scale[t], (128, ROWS)))
        for k in range(piece // 128):
            lanes = slice(k * 128, (k + 1) * 128)
            wide = stream_v[t * ROWS:(t + 1) * ROWS, lanes].astype(jnp.float32)
            value = wide * factor * gain_ref[:, lanes].astype(jnp.float32)
            normed_v[t * ROWS:(t + 1) * ROWS, lanes] = value.astype(jnp.bfloat16)
    normed_out = pltpu.make_async_copy(normed_v, normed_ref, out_sem.at[1])
    normed_out.start()
    normed_out.wait()
    stream_out.wait()


def fused(attention, activated, residual, out_tiles, down_tiles, norm_gain):
    tokens, width_a = attention.shape
    width_h = activated.shape[1]
    piece = residual.shape[1]
    devices = lax.axis_size("gx")
    chunks = tokens // ROWS
    half = COLB // 2
    bf16, f32 = jnp.bfloat16, jnp.float32
    anywhere = pl.BlockSpec(memory_space=pl.ANY)
    dma = pltpu.SemaphoreType.DMA
    shape = jax.ShapeDtypeStruct((tokens, piece), bf16)
    return pl.pallas_call(
        functools.partial(fused_kernel, devices),
        out_shape=(shape, shape),
        in_specs=[anywhere] * 5 + [pl.BlockSpec(memory_space=pltpu.VMEM)],
        out_specs=(anywhere, anywhere),
        scratch_shapes=[
            pltpu.VMEM((tokens, width_a), bf16),
            pltpu.VMEM((tokens, width_h), bf16),
            pltpu.VMEM((tokens, width_a), bf16),
            pltpu.VMEM((tokens, width_h), bf16),
            pltpu.VMEM((tokens, piece), bf16),
            pltpu.VMEM((SLOTS, width_a, piece), bf16),
            pltpu.VMEM((SLOTS, width_h, piece), bf16),
            pltpu.VMEM((COLB, tokens, piece), f32),
            pltpu.VMEM((half, ROWS, piece), bf16),
            pltpu.VMEM((chunks, half, ROWS, piece), bf16),
            pltpu.VMEM((half - 1, ROWS, piece), bf16),
            pltpu.VMEM((chunks, half - 1, ROWS, piece), bf16),
            pltpu.VMEM((ROWS, piece), f32),
            pltpu.VMEM((tokens, piece), bf16),
            pltpu.VMEM((tokens, piece), bf16),
            pltpu.VMEM((devices, chunks, 1, ROWS), f32),
            dma((3,)),
            dma((2, SLOTS)),
            dma((2, chunks)),
            dma((2, chunks)),
            dma((half,)),
            dma((chunks, half)),
            dma((half - 1,)),
            dma((chunks, half - 1)),
            dma((devices,)),
            dma((devices,)),
            dma((2,)),
        ],
        compiler_params=pltpu.CompilerParams(
            collective_id=0, has_side_effects=True, vmem_limit_bytes=63 * 1024 * 1024
        ),
        cost_estimate=pl.CostEstimate(
            flops=2 * tokens * 2 * (width_a + width_h) * COLB * piece,
            bytes_accessed=2 * (width_a + width_h) * COLB * piece * (chunks + 1),
            transcendentals=0,
        ),
    )(attention, activated, residual, out_tiles, down_tiles, norm_gain.reshape(1, piece))


def shifted(block, axis, distance):
    devices = range(lax.axis_size(axis))
    route = [((i - distance) % len(devices), i) for i in devices]
    return lax.ppermute(block, axis, route)


def from_partner(array, axis, stride):
    return lax.ppermute(array, axis, [(i, i ^ 1 << stride) for i in range(lax.axis_size(axis))])


def forward_move(pieces):
    return shifted((pieces[0], pieces[1]), "gx", COLB)


def body(attention, activated, residual, out_tiles, down_tiles, norm_gain):
    tile_out = out_tiles[0]
    tile_down = down_tiles[0]
    tok_rows = attention.shape[0]
    width_a = attention.shape[1]
    width_h = activated.shape[1]
    block_cols = tile_out.shape[1]
    shards = lax.axis_size("gx")
    row_groups = shards // COLB
    place = lax.axis_index("gx")
    own_group = place // COLB

    def contribute(carry, pieces, group_index):
        rows_out = lax.dynamic_slice_in_dim(tile_out, group_index * width_a, width_a, 0)
        rows_down = lax.dynamic_slice_in_dim(tile_down, group_index * width_h, width_h, 0)
        carry = carry + jnp.dot(pieces[0], rows_out, preferred_element_type=jnp.float32)
        return carry + jnp.dot(pieces[1], rows_down, preferred_element_type=jnp.float32)

    initial = jnp.zeros((tok_rows, block_cols), jnp.float32)
    own_pieces = (attention, activated)

    def advance_one(step, state):
        total, pieces = state
        total = contribute(total, pieces, (own_group - step) % row_groups)
        return (total, forward_move(pieces))

    carry, pieces = lax.fori_loop(0, row_groups - 1, advance_one, (initial, own_pieces))
    carry = contribute(carry, pieces, (own_group - row_groups + 1) % row_groups)
    levels = COLB.bit_length() - 1
    partial_value = carry
    for bit in range(levels - 1, -1, -1):
        half = partial_value.shape[1] // 2
        lower = partial_value[:, :half]
        upper = partial_value[:, half:]
        upper_side = place >> bit & 1 == 1
        keep = jnp.where(upper_side, upper, lower)
        sent = jnp.where(upper_side, lower, upper)
        partial_value = keep + from_partner(sent, "gx", bit)
    total = partial_value
    total = total + residual.astype(jnp.float32)
    stream = total.astype(jnp.bfloat16)
    wide = stream.astype(jnp.float32)
    local_sq = jnp.sum(wide * wide, axis=1)
    summed = lax.psum(local_sq, "gx")
    mean_square = summed[:, None] / D
    normed = wide * lax.rsqrt(mean_square + 1e-05) * norm_gain.astype(jnp.float32)[None, :]
    return (stream, normed.astype(jnp.bfloat16))


def solution(mesh):
    placed = (
        P("groups", "gx"),
        P("groups", "gx"),
        P("groups", "gx"),
        P("gx", None, None),
        P("gx", None, None),
        P("gx"),
    )
    two_groups = mesh.shape["gx"] == 2 * COLB
    return jax.shard_map(
        fused if two_groups else body,
        mesh=mesh,
        in_specs=placed,
        out_specs=(P("groups", "gx"), P("groups", "gx")),
        check_vma=False,
    )
```
